128 devices in a mesh: grp: 8 (over x, core), mem: 16 (over z, y).
Axes of the slice: x: 4, y: 4, z: 4, core: 2. Of those that a mesh axis runs over, the one named last changes fastest.
Arguments:
- history: bfloat16 [65536, 256], P(('grp', 'mem')), may hold values from -6 to 6
- tiles: bfloat16 [81920, 128, 128], P(('grp', 'mem')), may hold values from -0.0390625 to 0.0390625
- tile_row: int32 [81920], P(('grp', 'mem')), may hold values from 0 to 63
- tile_col: int32 [81920], P(('grp', 'mem')), may hold values from 0 to 63
- weight: bfloat16 [256, 256], replicated, may hold values from -0.375 to 0.375
- bias: float32 [256], replicated, may hold values from -3 to 3
- cotangent: bfloat16 [65536, 256], P(('grp', 'mem')), may hold values from -0.0234375 to 0.0234375
Outputs:
- activation: bfloat16 [65536, 256], P(('grp', 'mem'))
- weight_grad: float32 [256, 256], replicated
- bias_grad: float32 [256], replicated
The draws below stay inside these ranges and needn't reach their ends.
All inputs are finite; a program needn't handle non-finite values.
Results may differ from the reference program's by a relative error of at most 0.012.
Values may be sent and summed in bfloat16 or wider, within the bound.
A program may use at most 128 MiB of HBM per device.

```python
import math
import jax
import jax.numpy as jnp
import numpy as np
from jax import lax

H = 256
BS = 128
RB = 4
TILE_DEV = 640
NODES = 65536
TILES = 81920
N_GRP = 8
N_MEM = 16


def plant(result, rng, low, largest):
    longest = result.shape.index(max(result.shape))
    spots = []
    for shift in (0, 1):
        where = [jax.random.randint(jax.random.fold_in(rng, axis), (), 0, length) for axis, length in enumerate(result.shape)]
        where[longest] = (where[longest] + shift) % result.shape[longest]
        spots.append(tuple(where))
    return result.at[spots[0]].set(low).at[spots[1]].set(largest)


def block_scale(rng, extent, cuts, low, largest):
    loudness = 1.0
    for dim, shards_of in cuts:
        steps = jax.random.uniform(jax.random.fold_in(jax.random.fold_in(rng, 6), dim), (shards_of,), jnp.float32, low / len(cuts), largest / len(cuts))
        loudness = loudness * jnp.repeat(jnp.exp(steps), extent[dim] // shards_of).reshape((-1,) + (1,) * (len(extent) - 1 - dim))
    return loudness


def cumulative_ranks(amount, skew):
    weights = [(1 << 20) // math.isqrt(standing ** skew) + 1 for standing in range(1, amount + 1)]
    scale = 1 + sum(weights) // (1 << 30)
    return np.cumsum(np.array([max(1, weight // scale) for weight in weights]))


def skewed_ids(key, extent, amount, lean):
    listing = cumulative_ranks(amount, lean)
    lot = jax.random.randint(jax.random.fold_in(key, 1), extent, 0, int(listing[amount - 1]))
    standing = jnp.searchsorted(jnp.asarray(listing, jnp.int32), lot, side="right")
    return jax.random.permutation(jax.random.fold_in(key, 2), amount)[standing].astype(jnp.int32)


def bell_draw(stream_key, extent, width, bound, cuts=(), held_as=jnp.bfloat16):
    gain = block_scale(stream_key, extent, cuts, -0.22, 0.18) if cuts else 1.0
    array = jax.random.normal(stream_key, extent, jnp.float32) * width * gain
    return jnp.minimum(jnp.maximum(array, -bound), bound).astype(held_as)


def setup_inputs(seed: int = 0) -> dict:
    key_of = jax.random.split(jax.random.key(seed), 8)
    return {
        "history": bell_draw(key_of[0], (NODES, H), 1.0, 6.0, ((0, 128),)),
        "tiles": bell_draw(key_of[1], (TILES, BS, BS), (TILE_DEV * BS // RB) ** -0.5, 0.0390625, ((0, 128),)),
        "tile_row": plant(skewed_ids(key_of[2], (TILES,), RB * N_MEM, 2), jax.random.fold_in(key_of[2], 3), 0, (RB * N_MEM) - 1).astype(jnp.int32),
        "tile_col": plant(jax.random.randint(key_of[3], (TILES,), 0, RB * N_MEM), jax.random.fold_in(key_of[3], 1), 0, (RB * N_MEM) - 1).astype(jnp.int32),
        "weight": bell_draw(key_of[4], (H, H), H ** -0.5, 0.375),
        "bias": bell_draw(key_of[5], (H,), 0.5, 3.0, (), jnp.float32),
        "cotangent": bell_draw(key_of[6], (NODES, H), (1.0 / NODES ** 0.5), 0.0234375, ((0, 128),)),
    }


def reference(history, tiles, tile_row, tile_col, weight, bias, cotangent):
    nblk = N_MEM * RB
    hist = history.reshape(N_GRP, nblk, BS, H)
    group_tiles = tiles.reshape(N_GRP, N_MEM * TILE_DEV, BS, BS)
    rows_all = tile_row.reshape(N_GRP, N_MEM * TILE_DEV)
    cols_all = tile_col.reshape(N_GRP, N_MEM * TILE_DEV)
    step = math.gcd(TILE_DEV, 64)
    count = (N_MEM * TILE_DEV) // step

    def one_group(items):
        blocks, gtiles, grows, gcols = items

        def accumulate(dense, index):
            start = (index * step).astype(jnp.int32)
            piece = lax.dynamic_slice_in_dim(gtiles, start, step, 0).astype(jnp.float32)
            rows = lax.dynamic_slice_in_dim(grows, start, step, 0)
            cols = lax.dynamic_slice_in_dim(gcols, start, step, 0)
            picked = blocks[cols].astype(jnp.float32)
            part = jnp.einsum("tij,tjh->tih", piece, picked, precision=lax.Precision.HIGHEST)
            return dense + jax.ops.segment_sum(part, rows, num_segments=nblk), None

        dense, unused = lax.scan(accumulate, jnp.zeros((nblk, BS, H), jnp.float32), jnp.arange(count, dtype=jnp.int32))
        return dense

    dense = lax.map(one_group, (hist, group_tiles, rows_all, cols_all))
    merged = dense.reshape(NODES, H).astype(jnp.bfloat16)
    pre = jnp.dot(merged, weight, preferred_element_type=jnp.float32) + bias
    sig = jax.nn.sigmoid(pre)
    activation = (pre * sig).astype(jnp.bfloat16)
    slope = sig * (1.0 + pre * (1.0 - sig))
    masked = (cotangent.astype(jnp.float32) * slope).astype(jnp.bfloat16)
    weight_grad = jnp.dot(merged.T, masked, preferred_element_type=jnp.float32)
    bias_grad = jnp.sum(masked.astype(jnp.float32), axis=0)
    return activation, weight_grad, bias_grad
```

```python
import functools

import jax
import jax.numpy as jnp
from jax import lax
from jax.experimental import pallas as pl
from jax.experimental.pallas import tpu as pltpu
from jax.sharding import PartitionSpec as P

MESH = pl.DeviceIdType.MESH
SIDE = 4
MEM = SIDE * SIDE
GRP = 8
OWN = 4
BS = 128
H = 256
NBLK = MEM * OWN
TILES = 640
PAIRS = (TILES + NBLK) // 2
LANES = 768
UNROLL = 32
PIECE = H // MEM
WIDE = H + 128
BF16 = jnp.bfloat16
F32 = jnp.float32
I32 = jnp.int32


def matched(j):
    return -1 if j % 2 == 0 else 1


def wrap(d):
    d = d % SIDE
    return -1 if d == SIDE - 1 else d


def parent(j, df, ds):
    axis, d = (1, ds) if ds != 0 else (0, df)
    return axis, (matched(j) if d == 2 else d)


def children(j, df, ds):
    m = matched(j)
    if ds != 0:
        return [(1, -m)] if ds == m else []
    kids = [(1, 1), (1, -1)]
    if df == 0:
        kids += [(0, 1), (0, -1)]
    elif df == m:
        kids += [(0, -m)]
    return kids


SLOT = {}
for _j in range(OWN):
    for _df in (0, 1, -1, 2):
        for _ds in (0, 1, -1, 2):
            for _c in children(_j, _df, _ds):
                SLOT[(_j, _df, _ds) + _c] = len(SLOT)
NSEND = len(SLOT)


def sort_tiles(row, col, order, ends):
    r_sub = lax.broadcasted_iota(I32, (NBLK, TILES), 0)
    count = jnp.sum(jnp.where(r_sub == row, 1, 0), axis=1, keepdims=True)
    pairs = (count + 1) // 2
    before = lax.broadcasted_iota(I32, (NBLK, 128), 0)
    here = lax.broadcasted_iota(I32, (NBLK, 128), 1)
    start = jnp.sum(jnp.where(before < here, pairs, 0), axis=0, keepdims=True)
    mine = jnp.sum(jnp.where(before == here, pairs, 0), axis=0, keepdims=True)
    ends[0:1, :] = jnp.clip(jnp.where(mine > 0, start + mine - 1, PAIRS), 0, PAIRS)
    lane = lax.broadcasted_iota(I32, (128, 128), 1)
    sub = lax.broadcasted_iota(I32, (128, 128), 0)
    place = lax.broadcasted_iota(I32, (128, LANES), 1)
    other = lax.broadcasted_iota(I32, (128, TILES), 1)
    tile_at = jnp.zeros((1, LANES), I32)
    col_at = jnp.zeros((1, LANES), I32)
    first_at = jnp.zeros((1, LANES), I32)
    for a in range(TILES // 128):
        part = slice(a * 128, (a + 1) * 128)
        turn = lambda v: jnp.sum(jnp.where(lane == sub, v[:, part], 0), axis=1, keepdims=True)
        row_c = turn(row)
        col_c = turn(col)
        number = sub[:, 0:1] + a * 128
        rank = jnp.sum(
            jnp.where((row == row_c) & (other < number), 1, 0), axis=1, keepdims=True
        )
        begin = jnp.sum(jnp.where(lane == row_c, start, 0), axis=1, keepdims=True)
        at = place == 2 * begin + rank
        tile_at += jnp.sum(jnp.where(at, TILES - number, 0), axis=0, keepdims=True)
        col_at += jnp.sum(jnp.where(at, col_c, 0), axis=0, keepdims=True)
        first_at += jnp.sum(jnp.where(at & (rank == 0), 1, 0), axis=0, keepdims=True)
    order[0:1, :] = jnp.clip(TILES - tile_at, 0, TILES)
    order[1:2, :] = jnp.clip(col_at, 0, NBLK - 1)
    order[2:3, :] = 1 - first_at


def kernel(
    hist, tiles, row, col, weight, bias, cot,
    act, wgrad, bgrad,
    hbuf, tbuf, pbuf, acc, rbuf, order_v, ends_v, order_s, ends_s,
    w_v, cot_v, gsend, got1, send2, got2, got3,
    local_sem, s_gather, r_gather, s_sum, r_sum, s_1, r_1, s_2, r_2, s_3, r_3,
):
    me = lax.axis_index("mem")
    grp = lax.axis_index("grp")
    z, y = me // SIDE, lax.rem(me, SIDE)

    def mem_id(dz, dy):
        return lax.rem(z + dz + SIDE, SIDE) * SIDE + lax.rem(y + dy + SIDE, SIDE)

    def device(j, df, ds):
        return mem_id(ds, df) if j < 2 else mem_id(df, ds)

    def block(j, df, ds):
        return device(j, df, ds) * OWN + j

    def neighbour(j, axis, side):
        return device(j, side, 0) if axis == 0 else device(j, 0, side)

    mem_others = [lax.rem(me + k, MEM) for k in range(1, MEM)]
    grp_others = [lax.rem(grp + k, GRP) for k in range(1, GRP)]

    load_tiles = pltpu.make_async_copy(tiles, tbuf.at[pl.ds(0, TILES)], local_sem.at[0])
    load_w = pltpu.make_async_copy(weight, w_v, local_sem.at[1])
    load_cot = pltpu.make_async_copy(cot, cot_v, local_sem.at[2])
    keep = [
        pltpu.make_async_copy(hist.at[j], hbuf.at[me * OWN + j], local_sem.at[3 + j])
        for j in range(OWN)
    ]

    barrier = pltpu.get_barrier_semaphore()
    for o in mem_others:
        pl.semaphore_signal(barrier, inc=1, device_id={"mem": o}, device_id_type=MESH)
    for o in grp_others:
        pl.semaphore_signal(barrier, inc=1, device_id={"grp": o}, device_id_type=MESH)
    pl.semaphore_wait(barrier, MEM - 1 + GRP - 1)

    sends = []

    def send(j, df, ds, axis, side):
        b = block(j, df, ds)
        copy = pltpu.make_async_remote_copy(
            src_ref=hist.at[j] if df == 0 and ds == 0 else hbuf.at[b],
            dst_ref=hbuf.at[b],
            send_sem=s_gather.at[len(sends)],
            recv_sem=r_gather.at[b],
            device_id={"mem": neighbour(j, axis, side)},
            device_id_type=MESH,
        )
        copy.start()
        sends.append(copy)

    def arrive(j, df, ds):
        b = block(j, df, ds)
        axis, side = parent(j, df, ds)
        pltpu.make_async_remote_copy(
            src_ref=hbuf.at[b],
            dst_ref=hbuf.at[b],
            send_sem=s_gather.at[0],
            recv_sem=r_gather.at[b],
            device_id={"mem": neighbour(j, axis, side)},
            device_id_type=MESH,
        ).wait_recv()

    def pass_on(j, df, ds):
        kids = children(j, df, ds)
        for axis, side in sorted(kids):
            send(j, df, ds, axis, side)

    for part in (0, 1):
        for j in range(OWN):
            send(j, 0, 0, 0, -matched(j) if part == 0 else matched(j))
    for j in range(OWN):
        for side in (1, -1):
            send(j, 0, 0, 1, side)
    for c in keep:
        c.start()
    load_tiles.start()
    load_w.start()
    load_cot.start()

    for j in range(OWN):
        arrive(j, matched(j), 0)
        pass_on(j, matched(j), 0)
    for j in range(OWN):
        arrive(j, -matched(j), 0)
        pass_on(j, -matched(j), 0)

    sort_tiles(row[...], col[...], order_v, ends_v)
    to_s = [
        pltpu.make_async_copy(order_v, order_s, local_sem.at[7]),
        pltpu.make_async_copy(ends_v, ends_s, local_sem.at[8]),
    ]
    for c in to_s:
        c.start()

    for j in range(OWN):
        arrive(j, 0, matched(j))
        pass_on(j, 0, matched(j))
    for j in range(OWN):
        arrive(j, 2, 0)
        pass_on(j, 2, 0)
    for df in (1, -1, 2):
        for j in range(OWN):
            arrive(j, df, matched(j))
            pass_on(j, df, matched(j))
    tbuf[TILES] = jnp.zeros((BS, BS), BF16)
    pbuf[PAIRS] = jnp.zeros((BS, H), BF16)
    acc[...] = jnp.zeros((BS, H), F32)
    load_tiles.wait()
    load_w.wait()
    load_cot.wait()
    for c in keep:
        c.wait()
    for c in to_s:
        c.wait()
    for df in (0, 1, -1, 2):
        for j in range(OWN):
            arrive(j, df, -matched(j))
    for df in (0, 1, -1, 2):
        for j in range(OWN):
            arrive(j, df, 2)
    for c in sends:
        c.wait_send()

    def product(slot):
        left = [tbuf[order_s[0, 2 * slot + k]] for k in (0, 1)]
        right = [hbuf[order_s[1, 2 * slot + k]] for k in (0, 1)]
        return jnp.dot(
            jnp.concatenate(left, axis=1),
            jnp.concatenate(right, axis=0),
            preferred_element_type=F32,
        )

    def batch(q, _):
        parts = [product(q * UNROLL + u) for u in range(UNROLL)]
        total = acc[...]
        for u in range(UNROLL):
            slot = q * UNROLL + u
            total = parts[u] + total * order_s[2, 2 * slot].astype(F32)
            pbuf[slot] = total.astype(BF16)
        acc[...] = total
        return 0

    lax.fori_loop(0, PAIRS // UNROLL, batch, 0)

    own = hbuf
    sums = []

    def reduce_block(j, df, ds):
        b = block(j, df, ds)
        kids = children(j, df, ds)
        partial = pbuf[ends_s[0, b]]
        if kids:
            total = partial.astype(F32)
            for axis, side in kids:
                slot = SLOT[(j, df, ds, axis, side)]
                pltpu.make_async_remote_copy(
                    src_ref=own.at[b],
                    dst_ref=rbuf.at[slot],
                    send_sem=s_sum.at[0],
                    recv_sem=r_sum.at[slot],
                    device_id={"mem": neighbour(j, axis, side)},
                    device_id_type=MESH,
                ).wait_recv()
                total = total + rbuf[slot].astype(F32)
            if df == 0 and ds == 0:
                return total
            partial = total.astype(BF16)
        own[b] = partial
        axis, side = parent(j, df, ds)
        there = (df, wrap(ds - side)) if axis == 1 else (wrap(df - side), ds)
        slot = SLOT[(j,) + there + (axis, -side)]
        copy = pltpu.make_async_remote_copy(
            src_ref=own.at[b],
            dst_ref=rbuf.at[slot],
            send_sem=s_sum.at[len(sums)],
            recv_sem=r_sum.at[slot],
            device_id={"mem": neighbour(j, axis, side)},
            device_id_type=MESH,
        )
        copy.start()
        sums.append(copy)

    for df in (2, 1, -1, 0):
        for j in range(OWN):
            reduce_block(j, df, 2)
    for df in (2, 1, -1, 0):
        for j in range(OWN):
            reduce_block(j, df, -matched(j))
    for df in (2, 1, -1, 0):
        for j in range(OWN):
            reduce_block(j, df, matched(j))
    for j in range(OWN):
        reduce_block(j, 2, 0)
    for j in range(OWN):
        reduce_block(j, -matched(j), 0)
    for j in range(OWN):
        reduce_block(j, matched(j), 0)

    grad_sum = jnp.zeros((H, H), F32)
    bias_sum = jnp.zeros((1, H), F32)
    for j in range(OWN):
        merged = reduce_block(j, 0, 0).astype(BF16)
        pre = jnp.dot(merged, w_v[...], preferred_element_type=F32) + bias[...]
        sig = jax.nn.sigmoid(pre)
        nodes = slice(j * BS, (j + 1) * BS)
        act[nodes, :] = (pre * sig).astype(BF16)
        slope = sig * (1.0 + pre * (1.0 - sig))
        masked = (cot_v[nodes, :].astype(F32) * slope).astype(BF16)
        grad_sum = grad_sum + lax.dot_general(
            merged, masked, (((0,), (0,)), ((), ())), preferred_element_type=F32
        )
        bias_sum = bias_sum + jnp.sum(masked.astype(F32), axis=0, keepdims=True)

    line = lax.broadcasted_iota(I32, (PIECE, 128), 0)
    beside = jnp.where(
        line == 0, bias_sum[:, 0:128], jnp.where(line == 1, bias_sum[:, 128:256], 0.0)
    ).astype(BF16)
    for m in range(MEM):
        gsend[m, :, 0:H] = grad_sum[m * PIECE : (m + 1) * PIECE, :].astype(BF16)
        gsend[m, :, H:WIDE] = beside

    def to_mem(src, dst, s, r, k):
        return pltpu.make_async_remote_copy(
            src_ref=src, dst_ref=dst, send_sem=s.at[k], recv_sem=r.at[k],
            device_id={"mem": mem_others[k]}, device_id_type=MESH,
        )

    first = [to_mem(gsend.at[o], got1.at[me], s_1, r_1, k) for k, o in enumerate(mem_others)]
    for c in first:
        c.start()
    got1[me] = gsend[me]
    for c in first:
        c.wait_recv()
    total = got1[0].astype(F32)
    for m in range(1, MEM):
        total = total + got1[m].astype(F32)
    send2[...] = total.astype(BF16)
    second = [
        pltpu.make_async_remote_copy(
            src_ref=send2, dst_ref=got2.at[grp], send_sem=s_2.at[k], recv_sem=r_2.at[k],
            device_id={"grp": o}, device_id_type=MESH,
        )
        for k, o in enumerate(grp_others)
    ]
    for c in second:
        c.start()
    got2[grp] = send2[...]
    for c in second:
        c.wait_recv()
    total = got2[0].astype(F32)
    for g in range(1, GRP):
        total = total + got2[g].astype(F32)
    got3[me] = total[:, 0:H].astype(BF16)
    third = [to_mem(got3.at[me], got3.at[me], s_3, r_3, k) for k in range(MEM - 1)]
    for c in third:
        c.start()
    bgrad[:, 0:128] = total[0:1, H:WIDE]
    bgrad[:, 128:256] = total[1:2, H:WIDE]
    for c in sums + first + second:
        c.wait_send()
    for c in third:
        c.wait_recv()
    for m in range(MEM):
        wgrad[m * PIECE : (m + 1) * PIECE, :] = got3[m].astype(F32)
    for c in third:
        c.wait_send()


def per_device(history, tiles, tile_row, tile_col, weight, bias, cotangent):
    any_ref = pl.BlockSpec(memory_space=pl.ANY)
    vmem = pl.BlockSpec(memory_space=pltpu.VMEM)
    dma = pltpu.SemaphoreType.DMA
    nodes = history.shape[0]
    act, wgrad, bgrad = pl.pallas_call(
        kernel,
        out_shape=(
            jax.ShapeDtypeStruct((nodes, H), BF16),
            jax.ShapeDtypeStruct((H, H), F32),
            jax.ShapeDtypeStruct((1, H), F32),
        ),
        in_specs=[any_ref, any_ref, vmem, vmem, any_ref, vmem, any_ref],
        out_specs=(vmem, vmem, vmem),
        scratch_shapes=[
            pltpu.VMEM((NBLK, BS, H), BF16),
            pltpu.VMEM((TILES + 1, BS, BS), BF16),
            pltpu.VMEM((PAIRS + 1, BS, H), BF16),
            pltpu.VMEM((BS, H), F32),
            pltpu.VMEM((NSEND, BS, H), BF16),
            pltpu.VMEM((8, LANES), I32),
            pltpu.VMEM((8, 128), I32),
            pltpu.SMEM((8, LANES), I32),
            pltpu.SMEM((8, 128), I32),
            pltpu.VMEM((H, H), BF16),
            pltpu.VMEM((OWN * BS, H), BF16),
                pltpu.VMEM((MEM, PIECE, WIDE), BF16),
            pltpu.VMEM((MEM, PIECE, WIDE), BF16),
            pltpu.VMEM((PIECE, WIDE), BF16),
            pltpu.VMEM((GRP, PIECE, WIDE), BF16),
            pltpu.VMEM((MEM, PIECE, H), BF16),
            dma((9,)),
            dma((NSEND,)),
            dma((NBLK,)),
            dma((NSEND,)),
            dma((NSEND,)),
            dma((MEM - 1,)),
            dma((MEM - 1,)),
            dma((GRP - 1,)),
            dma((GRP - 1,)),
            dma((MEM - 1,)),
            dma((MEM - 1,)),
        ],
        compiler_params=pltpu.CompilerParams(
            collective_id=0, has_side_effects=True, vmem_limit_bytes=61 * 2**20
        ),
    )(
        history.reshape(OWN, BS, H),
        tiles,
        tile_row.reshape(1, TILES),
        tile_col.reshape(1, TILES),
        weight,
        bias.reshape(1, H),
        cotangent,
    )
    return act, wgrad, bgrad.reshape(H)


def solution(mesh):
    both = ("grp", "mem")
    placed = (
        P(both, None),
        P(both, None, None),
        P(both),
        P(both),
        P(),
        P(),
        P(both, None),
    )
    return jax.shard_map(
        per_device,
        mesh=mesh,
        in_specs=placed,
        out_specs=(P(both, None), P(), P()),
        check_vma=False,
    )
```

```python
import functools

import jax
import jax.numpy as jnp
from jax import lax
from jax.experimental import pallas as pl
from jax.experimental.pallas import tpu as pltpu
from jax.sharding import PartitionSpec as P

MESH = pl.DeviceIdType.MESH
SIDE = 4
MEM = SIDE * SIDE
GRP = 8
OWN = 4
BS = 128
H = 256
NBLK = MEM * OWN
TILES = 640
PAIRS = (TILES + NBLK) // 2
LANES = 768
UNROLL = 32
PIECE = H // MEM
WIDE = H + 128
BF16 = jnp.bfloat16
F32 = jnp.float32
I32 = jnp.int32


def matched(j):
    return -1 if j % 2 == 0 else 1


def wrap(d):
    d = d % SIDE
    return -1 if d == SIDE - 1 else d


def parent(j, df, ds):
    axis, d = (1, ds) if ds != 0 else (0, df)
    return axis, (matched(j) if d == 2 else d)


def children(j, df, ds):
    m = matched(j)
    if ds != 0:
        return [(1, -m)] if ds == m else []
    kids = [(1, 1), (1, -1)]
    if df == 0:
        kids += [(0, 1), (0, -1)]
    elif df == m:
        kids += [(0, -m)]
    return kids


SLOT = {}
for _j in range(OWN):
    for _df in (0, 1, -1, 2):
        for _ds in (0, 1, -1, 2):
            for _c in children(_j, _df, _ds):
                SLOT[(_j, _df, _ds) + _c] = len(SLOT)
NSEND = len(SLOT)


def sort_tiles(row, col, order, ends):
    r_sub = lax.broadcasted_iota(I32, (NBLK, TILES), 0)
    count = jnp.sum(jnp.where(r_sub == row, 1, 0), axis=1, keepdims=True)
    pairs = (count + 1) // 2
    before = lax.broadcasted_iota(I32, (NBLK, 128), 0)
    here = lax.broadcasted_iota(I32, (NBLK, 128), 1)
    start = jnp.sum(jnp.where(before < here, pairs, 0), axis=0, keepdims=True)
    mine = jnp.sum(jnp.where(before == here, pairs, 0), axis=0, keepdims=True)
    ends[0:1, :] = jnp.clip(jnp.where(mine > 0, start + mine - 1, PAIRS), 0, PAIRS)
    lane = lax.broadcasted_iota(I32, (128, 128), 1)
    sub = lax.broadcasted_iota(I32, (128, 128), 0)
    place = lax.broadcasted_iota(I32, (128, LANES), 1)
    other = lax.broadcasted_iota(I32, (128, TILES), 1)
    tile_at = jnp.zeros((1, LANES), I32)
    col_at = jnp.zeros((1, LANES), I32)
    first_at = jnp.zeros((1, LANES), I32)
    for a in range(TILES // 128):
        part = slice(a * 128, (a + 1) * 128)
        turn = lambda v: jnp.sum(jnp.where(lane == sub, v[:, part], 0), axis=1, keepdims=True)
        row_c = turn(row)
        col_c = turn(col)
        number = sub[:, 0:1] + a * 128
        rank = jnp.sum(
            jnp.where((row == row_c) & (other < number), 1, 0), axis=1, keepdims=True
        )
        begin = jnp.sum(jnp.where(lane == row_c, start, 0), axis=1, keepdims=True)
        at = place == 2 * begin + rank
        tile_at += jnp.sum(jnp.where(at, TILES - number, 0), axis=0, keepdims=True)
        col_at += jnp.sum(jnp.where(at, col_c, 0), axis=0, keepdims=True)
        first_at += jnp.sum(jnp.where(at & (rank == 0), 1, 0), axis=0, keepdims=True)
    order[0:1, :] = jnp.clip(TILES - tile_at, 0, TILES)
    order[1:2, :] = jnp.clip(col_at, 0, NBLK - 1)
    order[2:3, :] = 1 - first_at


def kernel(
    hist, tiles, row, col, weight, bias, cot,
    act, wgrad, bgrad,
    hbuf, tbuf, pbuf, acc, rbuf, order_v, ends_v, order_s, ends_s,
    w_v, cot_v, gsend, got1, send2, got2, got3,
    local_sem, s_gather, r_gather, s_sum, r_sum, s_1, r_1, s_2, r_2, s_3, r_3,
):
    me = lax.axis_index("mem")
    grp = lax.axis_index("grp")
    z, y = me // SIDE, lax.rem(me, SIDE)

    def mem_id(dz, dy):
        return lax.rem(z + dz + SIDE, SIDE) * SIDE + lax.rem(y + dy + SIDE, SIDE)

    def device(j, df, ds):
        return mem_id(ds, df) if j < 2 else mem_id(df, ds)

    def block(j, df, ds):
        return device(j, df, ds) * OWN + j

    def neighbour(j, axis, side):
        return device(j, side, 0) if axis == 0 else device(j, 0, side)

    mem_others = [lax.rem(me + k, MEM) for k in range(1, MEM)]
    grp_others = [lax.rem(grp + k, GRP) for k in range(1, GRP)]

    load_tiles = pltpu.make_async_copy(tiles, tbuf.at[pl.ds(0, TILES)], local_sem.at[0])
    load_w = pltpu.make_async_copy(weight, w_v, local_sem.at[1])
    load_cot = pltpu.make_async_copy(cot, cot_v, local_sem.at[2])
    keep = [
        pltpu.make_async_copy(hist.at[j], hbuf.at[me * OWN + j], local_sem.at[3 + j])
        for j in range(OWN)
    ]

    barrier = pltpu.get_barrier_semaphore()
    for o in mem_others:
        pl.semaphore_signal(barrier, inc=1, device_id={"mem": o}, device_id_type=MESH)
    for o in grp_others:
        pl.semaphore_signal(barrier, inc=1, device_id={"grp": o}, device_id_type=MESH)
    for c in keep:
        c.start()
    pl.semaphore_wait(barrier, MEM - 1 + GRP - 1)

    sends = []

    def send(j, df, ds, axis, side):
        b = block(j, df, ds)
        copy = pltpu.make_async_remote_copy(
            src_ref=hist.at[j] if df == 0 and ds == 0 else hbuf.at[b],
            dst_ref=hbuf.at[b],
            send_sem=s_gather.at[len(sends)],
            recv_sem=r_gather.at[b],
            device_id={"mem": neighbour(j, axis, side)},
            device_id_type=MESH,
        )
        copy.start()
        sends.append(copy)

    def arrive(j, df, ds):
        b = block(j, df, ds)
        axis, side = parent(j, df, ds)
        pltpu.make_async_remote_copy(
            src_ref=hbuf.at[b],
            dst_ref=hbuf.at[b],
            send_sem=s_gather.at[0],
            recv_sem=r_gather.at[b],
            device_id={"mem": neighbour(j, axis, side)},
            device_id_type=MESH,
        ).wait_recv()

    def pass_on(j, df, ds):
        kids = children(j, df, ds)
        for axis, side in sorted(kids):
            send(j, df, ds, axis, side)

    for part in (0, 1):
        for j in range(OWN):
            send(j, 0, 0, 0, -matched(j) if part == 0 else matched(j))
    for j in range(OWN):
        for side in (1, -1):
            send(j, 0, 0, 1, side)
    load_tiles.start()
    load_w.start()
    load_cot.start()

    for j in range(OWN):
        arrive(j, matched(j), 0)
        pass_on(j, matched(j), 0)
    for j in range(OWN):
        arrive(j, -matched(j), 0)
        pass_on(j, -matched(j), 0)

    sort_tiles(row[...].reshape(1, TILES), col[...].reshape(1, TILES), order_v, ends_v)
    to_s = [
        pltpu.make_async_copy(order_v, order_s, local_sem.at[7]),
        pltpu.make_async_copy(ends_v, ends_s, local_sem.at[8]),
    ]
    for c in to_s:
        c.start()

    for j in range(OWN):
        arrive(j, 0, matched(j))
        pass_on(j, 0, matched(j))
    for j in range(OWN):
        arrive(j, 2, 0)
        pass_on(j, 2, 0)
    for df in (1, -1, 2):
        for j in range(OWN):
            arrive(j, df, matched(j))
            pass_on(j, df, matched(j))
    tbuf[TILES] = jnp.zeros((BS, BS), BF16)
    pbuf[PAIRS] = jnp.zeros((BS, H), BF16)
    acc[...] = jnp.zeros((BS, H), F32)
    load_tiles.wait()
    load_w.wait()
    load_cot.wait()
    for c in keep:
        c.wait()
    for c in to_s:
        c.wait()
    for df in (0, 1, -1, 2):
        for j in range(OWN):
            arrive(j, df, -matched(j))
    for df in (0, 1, -1, 2):
        for j in range(OWN):
            arrive(j, df, 2)

    def product(slot):
        left = [tbuf[order_s[0, 2 * slot + k]] for k in (0, 1)]
        right = [hbuf[order_s[1, 2 * slot + k]] for k in (0, 1)]
        return jnp.dot(
            jnp.concatenate(left, axis=1),
            jnp.concatenate(right, axis=0),
            preferred_element_type=F32,
        )

    def batch(q, _):
        parts = [product(q * UNROLL + u) for u in range(UNROLL)]
        total = acc[...]
        for u in range(UNROLL):
            slot = q * UNROLL + u
            total = parts[u] + total * order_s[2, 2 * slot].astype(F32)
            pbuf[slot] = total.astype(BF16)
        acc[...] = total
        return 0

    lax.fori_loop(0, PAIRS // UNROLL, batch, 0)
    for c in sends:
        c.wait_send()

    own = hbuf
    sums = []

    def reduce_block(j, df, ds):
        b = block(j, df, ds)
        kids = children(j, df, ds)
        partial = pbuf[ends_s[0, b]]
        if kids:
            total = partial.astype(F32)
            for axis, side in kids:
                slot = SLOT[(j, df, ds, axis, side)]
                pltpu.make_async_remote_copy(
                    src_ref=own.at[b],
                    dst_ref=rbuf.at[slot],
                    send_sem=s_sum.at[0],
                    recv_sem=r_sum.at[slot],
                    device_id={"mem": neighbour(j, axis, side)},
                    device_id_type=MESH,
                ).wait_recv()
                total = total + rbuf[slot].astype(F32)
            if df == 0 and ds == 0:
                return total
            partial = total.astype(BF16)
        own[b] = partial
        axis, side = parent(j, df, ds)
        there = (df, wrap(ds - side)) if axis == 1 else (wrap(df - side), ds)
        slot = SLOT[(j,) + there + (axis, -side)]
        copy = pltpu.make_async_remote_copy(
            src_ref=own.at[b],
            dst_ref=rbuf.at[slot],
            send_sem=s_sum.at[len(sums)],
            recv_sem=r_sum.at[slot],
            device_id={"mem": neighbour(j, axis, side)},
            device_id_type=MESH,
        )
        copy.start()
        sums.append(copy)

    for df in (2, 1, -1, 0):
        for j in range(OWN):
            reduce_block(j, df, 2)
    for df in (2, 1, -1, 0):
        for j in range(OWN):
            reduce_block(j, df, -matched(j))
    for df in (2, 1, -1, 0):
        for j in range(OWN):
            reduce_block(j, df, matched(j))
    for j in range(OWN):
        reduce_block(j, 2, 0)
    for j in range(OWN):
        reduce_block(j, -matched(j), 0)
    for j in range(OWN):
        reduce_block(j, matched(j), 0)

    grad_sum = jnp.zeros((H, H), F32)
    bias_sum = jnp.zeros((1, H), F32)
    for j in range(OWN):
        merged = reduce_block(j, 0, 0).astype(BF16)
        pre = jnp.dot(merged, w_v[...], preferred_element_type=F32) + bias[...]
        sig = jax.nn.sigmoid(pre)
        nodes = slice(j * BS, (j + 1) * BS)
        act[nodes, :] = (pre * sig).astype(BF16)
        slope = sig * (1.0 + pre * (1.0 - sig))
        masked = (cot_v[nodes, :].astype(F32) * slope).astype(BF16)
        grad_sum = grad_sum + lax.dot_general(
            merged, masked, (((0,), (0,)), ((), ())), preferred_element_type=F32
        )
        bias_sum = bias_sum + jnp.sum(masked.astype(F32), axis=0, keepdims=True)

    line = lax.broadcasted_iota(I32, (PIECE, 128), 0)
    beside = jnp.where(
        line == 0, bias_sum[:, 0:128], jnp.where(line == 1, bias_sum[:, 128:256], 0.0)
    ).astype(BF16)
    for m in range(MEM):
        gsend[m, :, 0:H] = grad_sum[m * PIECE : (m + 1) * PIECE, :].astype(BF16)
        gsend[m, :, H:WIDE] = beside

    def to_mem(src, dst, s, r, k):
        return pltpu.make_async_remote_copy(
            src_ref=src, dst_ref=dst, send_sem=s.at[k], recv_sem=r.at[k],
            device_id={"mem": mem_others[k]}, device_id_type=MESH,
        )

    first = [to_mem(gsend.at[o], got1.at[me], s_1, r_1, k) for k, o in enumerate(mem_others)]
    for c in first:
        c.start()
    got1[me] = gsend[me]
    for c in first:
        c.wait_recv()
    total = got1[0].astype(F32)
    for m in range(1, MEM):
        total = total + got1[m].astype(F32)
    send2[...] = total.astype(BF16)
    second = [
        pltpu.make_async_remote_copy(
            src_ref=send2, dst_ref=got2.at[grp], send_sem=s_2.at[k], recv_sem=r_2.at[k],
            device_id={"grp": o}, device_id_type=MESH,
        )
        for k, o in enumerate(grp_others)
    ]
    for c in second:
        c.start()
    got2[grp] = send2[...]
    for c in second:
        c.wait_recv()
    total = got2[0].astype(F32)
    for g in range(1, GRP):
        total = total + got2[g].astype(F32)
    got3[me] = total[:, 0:H].astype(BF16)
    third = [to_mem(got3.at[me], got3.at[me], s_3, r_3, k) for k in range(MEM - 1)]
    for c in third:
        c.start()
    bgrad[:, 0:128] = total[0:1, H:WIDE]
    bgrad[:, 128:256] = total[1:2, H:WIDE]
    for c in sums + first + second:
        c.wait_send()
    for c in third:
        c.wait_recv()
    wgrad[...] = got3[...]
    for c in third:
        c.wait_send()


def finish(act, pieces, bgrad, act_out, wgrad_out, bgrad_out):
    act_out[...] = act[...]
    for m in range(MEM):
        wgrad_out[m * PIECE : (m + 1) * PIECE, :] = pieces[m].astype(F32)
    bgrad_out[...] = bgrad[...]


def per_device(history, tiles, tile_row, tile_col, weight, bias, cotangent):
    any_ref = pl.BlockSpec(memory_space=pl.ANY)
    vmem = pl.BlockSpec(memory_space=pltpu.VMEM)
    dma = pltpu.SemaphoreType.DMA
    nodes = history.shape[0]
    act, wgrad, bgrad = pl.pallas_call(
        kernel,
        out_shape=(
            jax.ShapeDtypeStruct((nodes, H), BF16),
            jax.ShapeDtypeStruct((MEM, PIECE, H), BF16),
            jax.ShapeDtypeStruct((1, H), F32),
        ),
        in_specs=[any_ref, any_ref, vmem, vmem, any_ref, vmem, any_ref],
        out_specs=(vmem, vmem, vmem),
        scratch_shapes=[
            pltpu.VMEM((NBLK, BS, H), BF16),
            pltpu.VMEM((TILES + 1, BS, BS), BF16),
            pltpu.VMEM((PAIRS + 1, BS, H), BF16),
            pltpu.VMEM((BS, H), F32),
            pltpu.VMEM((NSEND, BS, H), BF16),
            pltpu.VMEM((8, LANES), I32),
            pltpu.VMEM((8, 128), I32),
            pltpu.SMEM((8, LANES), I32),
            pltpu.SMEM((8, 128), I32),
            pltpu.VMEM((H, H), BF16),
            pltpu.VMEM((OWN * BS, H), BF16),
                pltpu.VMEM((MEM, PIECE, WIDE), BF16),
            pltpu.VMEM((MEM, PIECE, WIDE), BF16),
            pltpu.VMEM((PIECE, WIDE), BF16),
            pltpu.VMEM((GRP, PIECE, WIDE), BF16),
            pltpu.VMEM((MEM, PIECE, H), BF16),
            dma((9,)),
            dma((NSEND,)),
            dma((NBLK,)),
            dma((NSEND,)),
            dma((NSEND,)),
            dma((MEM - 1,)),
            dma((MEM - 1,)),
            dma((GRP - 1,)),
            dma((GRP - 1,)),
            dma((MEM - 1,)),
            dma((MEM - 1,)),
        ],
        compiler_params=pltpu.CompilerParams(
            collective_id=0, has_side_effects=True, vmem_limit_bytes=61 * 2**20
        ),
    )(
        history.reshape(OWN, BS, H),
        tiles,
        tile_row,
        tile_col,
        weight,
        bias.reshape(1, H),
        cotangent,
    )
    act, wgrad, bgrad = pl.pallas_call(
        finish,
        out_shape=(
            jax.ShapeDtypeStruct((nodes, H), BF16),
            jax.ShapeDtypeStruct((H, H), F32),
            jax.ShapeDtypeStruct((1, H), F32),
        ),
        in_specs=[vmem, vmem, vmem],
        out_specs=(vmem, vmem, vmem),
        compiler_params=pltpu.CompilerParams(vmem_limit_bytes=61 * 2**20),
    )(act, wgrad, bgrad)
    return act, wgrad, bgrad.reshape(H)


def solution(mesh):
    both = ("grp", "mem")
    placed = (
        P(both, None),
        P(both, None, None),
        P(both),
        P(both),
        P(),
        P(),
        P(both, None),
    )
    return jax.shard_map(
        per_device,
        mesh=mesh,
        in_specs=placed,
        out_specs=(P(both, None), P(), P()),
        check_vma=False,
    )
```

```python
import functools

import jax
import jax.numpy as jnp
from jax import lax
from jax.experimental import pallas as pl
from jax.experimental.pallas import tpu as pltpu
from jax.sharding import PartitionSpec as P

MESH = pl.DeviceIdType.MESH
SIDE = 4
MEM = SIDE * SIDE
GRP = 8
OWN = 4
BS = 128
H = 256
NBLK = MEM * OWN
TILES = 640
PAIRS = (TILES + NBLK) // 2
LANES = 768
UNROLL = 32
PIECE = H // MEM
WIDE = H + 128
BF16 = jnp.bfloat16
F32 = jnp.float32
I32 = jnp.int32


def matched(j):
    return -1 if j % 2 == 0 else 1


def wrap(d):
    d = d % SIDE
    return -1 if d == SIDE - 1 else d


def parent(j, df, ds):
    axis, d = (1, ds) if ds != 0 else (0, df)
    return axis, (matched(j) if d == 2 else d)


def children(j, df, ds):
    m = matched(j)
    if ds != 0:
        return [(1, -m)] if ds == m else []
    kids = [(1, 1), (1, -1)]
    if df == 0:
        kids += [(0, 1), (0, -1)]
    elif df == m:
        kids += [(0, -m)]
    return kids


SLOT = {}
for _j in range(OWN):
    for _df in (0, 1, -1, 2):
        for _ds in (0, 1, -1, 2):
            for _c in children(_j, _df, _ds):
                SLOT[(_j, _df, _ds) + _c] = len(SLOT)
NSEND = len(SLOT)


def sort_tiles(row, col, order, ends):
    r_sub = lax.broadcasted_iota(I32, (NBLK, TILES), 0)
    count = jnp.sum(jnp.where(r_sub == row, 1, 0), axis=1, keepdims=True)
    pairs = (count + 1) // 2
    before = lax.broadcasted_iota(I32, (NBLK, 128), 0)
    here = lax.broadcasted_iota(I32, (NBLK, 128), 1)
    start = jnp.sum(jnp.where(before < here, pairs, 0), axis=0, keepdims=True)
    mine = jnp.sum(jnp.where(before == here, pairs, 0), axis=0, keepdims=True)
    ends[0:1, :] = jnp.clip(jnp.where(mine > 0, start + mine - 1, PAIRS), 0, PAIRS)
    lane = lax.broadcasted_iota(I32, (128, 128), 1)
    sub = lax.broadcasted_iota(I32, (128, 128), 0)
    place = lax.broadcasted_iota(I32, (128, LANES), 1)
    other = lax.broadcasted_iota(I32, (128, TILES), 1)
    tile_at = jnp.zeros((1, LANES), I32)
    col_at = jnp.zeros((1, LANES), I32)
    first_at = jnp.zeros((1, LANES), I32)
    for a in range(TILES // 128):
        part = slice(a * 128, (a + 1) * 128)
        turn = lambda v: jnp.sum(jnp.where(lane == sub, v[:, part], 0), axis=1, keepdims=True)
        row_c = turn(row)
        col_c = turn(col)
        number = sub[:, 0:1] + a * 128
        rank = jnp.sum(
            jnp.where((row == row_c) & (other < number), 1, 0), axis=1, keepdims=True
        )
        begin = jnp.sum(jnp.where(lane == row_c, start, 0), axis=1, keepdims=True)
        at = place == 2 * begin + rank
        tile_at += jnp.sum(jnp.where(at, TILES - number, 0), axis=0, keepdims=True)
        col_at += jnp.sum(jnp.where(at, col_c, 0), axis=0, keepdims=True)
        first_at += jnp.sum(jnp.where(at & (rank == 0), 1, 0), axis=0, keepdims=True)
    order[0:1, :] = jnp.clip(TILES - tile_at, 0, TILES)
    order[1:2, :] = jnp.clip(col_at, 0, NBLK - 1)
    order[2:3, :] = 1 - first_at


def kernel(
    hist, tiles, row, col, weight, bias, cot,
    act, wgrad, bgrad,
    hbuf, tbuf, pbuf, acc, rbuf, order_v, ends_v, order_s, ends_s,
    w_v, cot_v, gsend, got1, send2, got2, got3,
    local_sem, s_gather, r_gather, s_sum, r_sum, s_1, r_1, s_2, r_2, s_3, r_3,
):
    me = lax.axis_index("mem")
    grp = lax.axis_index("grp")
    z, y = me // SIDE, lax.rem(me, SIDE)

    def mem_id(dz, dy):
        return lax.rem(z + dz + SIDE, SIDE) * SIDE + lax.rem(y + dy + SIDE, SIDE)

    def device(j, df, ds):
        return mem_id(ds, df) if j < 2 else mem_id(df, ds)

    def block(j, df, ds):
        return device(j, df, ds) * OWN + j

    def neighbour(j, axis, side):
        return device(j, side, 0) if axis == 0 else device(j, 0, side)

    mem_others = [lax.rem(me + k, MEM) for k in range(1, MEM)]
    grp_others = [lax.rem(grp + k, GRP) for k in range(1, GRP)]

    load_tiles = pltpu.make_async_copy(tiles, tbuf.at[pl.ds(0, TILES)], local_sem.at[0])
    load_w = pltpu.make_async_copy(weight, w_v, local_sem.at[1])
    load_cot = pltpu.make_async_copy(cot, cot_v, local_sem.at[2])
    keep = [
        pltpu.make_async_copy(hist.at[j], hbuf.at[me * OWN + j], local_sem.at[3 + j])
        for j in range(OWN)
    ]

    barrier = pltpu.get_barrier_semaphore()
    for o in mem_others:
        pl.semaphore_signal(barrier, inc=1, device_id={"mem": o}, device_id_type=MESH)
    for o in grp_others:
        pl.semaphore_signal(barrier, inc=1, device_id={"grp": o}, device_id_type=MESH)
    for c in keep:
        c.start()
    pl.semaphore_wait(barrier, MEM - 1 + GRP - 1)

    sends = []

    def send(j, df, ds, axis, side):
        b = block(j, df, ds)
        copy = pltpu.make_async_remote_copy(
            src_ref=hist.at[j] if df == 0 and ds == 0 else hbuf.at[b],
            dst_ref=hbuf.at[b],
            send_sem=s_gather.at[len(sends)],
            recv_sem=r_gather.at[b],
            device_id={"mem": neighbour(j, axis, side)},
            device_id_type=MESH,
        )
        copy.start()
        sends.append(copy)

    def arrive(j, df, ds):
        b = block(j, df, ds)
        axis, side = parent(j, df, ds)
        pltpu.make_async_remote_copy(
            src_ref=hbuf.at[b],
            dst_ref=hbuf.at[b],
            send_sem=s_gather.at[0],
            recv_sem=r_gather.at[b],
            device_id={"mem": neighbour(j, axis, side)},
            device_id_type=MESH,
        ).wait_recv()

    def pass_on(j, df, ds):
        kids = children(j, df, ds)
        for axis, side in sorted(kids):
            send(j, df, ds, axis, side)

    for part in (0, 1):
        for j in range(OWN):
            send(j, 0, 0, 0, -matched(j) if part == 0 else matched(j))
    for j in range(OWN):
        for side in (1, -1):
            send(j, 0, 0, 1, side)
    load_tiles.start()
    load_w.start()
    load_cot.start()

    for j in range(OWN):
        arrive(j, matched(j), 0)
        pass_on(j, matched(j), 0)
    for j in range(OWN):
        arrive(j, -matched(j), 0)
        pass_on(j, -matched(j), 0)

    sort_tiles(row[...].reshape(1, TILES), col[...].reshape(1, TILES), order_v, ends_v)
    to_s = [
        pltpu.make_async_copy(order_v, order_s, local_sem.at[7]),
        pltpu.make_async_copy(ends_v, ends_s, local_sem.at[8]),
    ]
    for c in to_s:
        c.start()

    for j in range(OWN):
        arrive(j, 0, matched(j))
        pass_on(j, 0, matched(j))
    for j in range(OWN):
        arrive(j, 2, 0)
        pass_on(j, 2, 0)
    for df in (1, -1, 2):
        for j in range(OWN):
            arrive(j, df, matched(j))
            pass_on(j, df, matched(j))
    tbuf[TILES] = jnp.zeros((BS, BS), BF16)
    pbuf[PAIRS] = jnp.zeros((BS, H), BF16)
    acc[...] = jnp.zeros((BS, H), F32)
    load_tiles.wait()
    load_w.wait()
    load_cot.wait()
    for c in keep:
        c.wait()
    for c in to_s:
        c.wait()
    for df in (0, 1, -1, 2):
        for j in range(OWN):
            arrive(j, df, -matched(j))
    for df in (0, 1, -1, 2):
        for j in range(OWN):
            arrive(j, df, 2)

    def product(slot):
        left = [tbuf[order_s[0, 2 * slot + k]] for k in (0, 1)]
        right = [hbuf[order_s[1, 2 * slot + k]] for k in (0, 1)]
        return jnp.dot(
            jnp.concatenate(left, axis=1),
            jnp.concatenate(right, axis=0),
            preferred_element_type=F32,
        )

    def batch(q, _):
        parts = [product(q * UNROLL + u) for u in range(UNROLL)]
        total = acc[...]
        for u in range(UNROLL):
            slot = q * UNROLL + u
            total = parts[u] + total * order_s[2, 2 * slot].astype(F32)
            pbuf[slot] = total.astype(BF16)
        acc[...] = total
        return 0

    lax.fori_loop(0, PAIRS // UNROLL, batch, 0)
    for c in sends:
        c.wait_send()

    own = hbuf
    sums = []

    def reduce_block(j, df, ds):
        b = block(j, df, ds)
        kids = children(j, df, ds)
        partial = pbuf[ends_s[0, b]]
        if kids:
            total = partial.astype(F32)
            for axis, side in kids:
                slot = SLOT[(j, df, ds, axis, side)]
                pltpu.make_async_remote_copy(
                    src_ref=own.at[b],
                    dst_ref=rbuf.at[slot],
                    send_sem=s_sum.at[0],
                    recv_sem=r_sum.at[slot],
                    device_id={"mem": neighbour(j, axis, side)},
                    device_id_type=MESH,
                ).wait_recv()
                total = total + rbuf[slot].astype(F32)
            if df == 0 and ds == 0:
                return total
            partial = total.astype(BF16)
        own[b] = partial
        axis, side = parent(j, df, ds)
        there = (df, wrap(ds - side)) if axis == 1 else (wrap(df - side), ds)
        slot = SLOT[(j,) + there + (axis, -side)]
        copy = pltpu.make_async_remote_copy(
            src_ref=own.at[b],
            dst_ref=rbuf.at[slot],
            send_sem=s_sum.at[len(sums)],
            recv_sem=r_sum.at[slot],
            device_id={"mem": neighbour(j, axis, side)},
            device_id_type=MESH,
        )
        copy.start()
        sums.append(copy)

    for near in (2, 1, -1, 0):
        for j in range(OWN):
            reduce_block(j, near if near == 2 else near * matched(j), 2)
    for near in (2, 1, -1, 0):
        for j in range(OWN):
            reduce_block(j, near if near == 2 else near * matched(j), -matched(j))
        for j in range(OWN):
            reduce_block(j, near if near == 2 else near * matched(j), matched(j))
        if near != 2:
            for j in range(OWN):
                reduce_block(j, {1: 2, -1: matched(j), 0: -matched(j)}[near], 0)

    grad_sum = jnp.zeros((H, H), F32)
    bias_sum = jnp.zeros((1, H), F32)
    for j in range(OWN):
        merged = reduce_block(j, 0, 0).astype(BF16)
        pre = jnp.dot(merged, w_v[...], preferred_element_type=F32) + bias[...]
        sig = jax.nn.sigmoid(pre)
        nodes = slice(j * BS, (j + 1) * BS)
        act[nodes, :] = (pre * sig).astype(BF16)
        slope = sig * (1.0 + pre * (1.0 - sig))
        masked = (cot_v[nodes, :].astype(F32) * slope).astype(BF16)
        grad_sum = grad_sum + lax.dot_general(
            merged, masked, (((0,), (0,)), ((), ())), preferred_element_type=F32
        )
        bias_sum = bias_sum + jnp.sum(masked.astype(F32), axis=0, keepdims=True)

    line = lax.broadcasted_iota(I32, (PIECE, 128), 0)
    beside = jnp.where(
        line == 0, bias_sum[:, 0:128], jnp.where(line == 1, bias_sum[:, 128:256], 0.0)
    ).astype(BF16)
    for m in range(MEM):
        gsend[m, :, 0:H] = grad_sum[m * PIECE : (m + 1) * PIECE, :].astype(BF16)
        gsend[m, :, H:WIDE] = beside

    def to_mem(src, dst, s, r, k):
        return pltpu.make_async_remote_copy(
            src_ref=src, dst_ref=dst, send_sem=s.at[k], recv_sem=r.at[k],
            device_id={"mem": mem_others[k]}, device_id_type=MESH,
        )

    first = [to_mem(gsend.at[o], got1.at[me], s_1, r_1, k) for k, o in enumerate(mem_others)]
    for c in first:
        c.start()
    got1[me] = gsend[me]
    for c in first:
        c.wait_recv()
    total = got1[0].astype(F32)
    for m in range(1, MEM):
        total = total + got1[m].astype(F32)
    send2[...] = total.astype(BF16)
    second = [
        pltpu.make_async_remote_copy(
            src_ref=send2, dst_ref=got2.at[grp], send_sem=s_2.at[k], recv_sem=r_2.at[k],
            device_id={"grp": o}, device_id_type=MESH,
        )
        for k, o in enumerate(grp_others)
    ]
    for c in second:
        c.start()
    got2[grp] = send2[...]
    for c in second:
        c.wait_recv()
    total = got2[0].astype(F32)
    for g in range(1, GRP):
        total = total + got2[g].astype(F32)
    got3[me] = total[:, 0:H].astype(BF16)
    third = [to_mem(got3.at[me], got3.at[me], s_3, r_3, k) for k in range(MEM - 1)]
    for c in third:
        c.start()
    bgrad[:, 0:128] = total[0:1, H:WIDE]
    bgrad[:, 128:256] = total[1:2, H:WIDE]
    for c in sums + first + second:
        c.wait_send()
    for c in third:
        c.wait_recv()
    wgrad[...] = got3[...]
    for c in third:
        c.wait_send()


def finish(act, pieces, bgrad, act_out, wgrad_out, bgrad_out):
    act_out[...] = act[...]
    for m in range(MEM):
        wgrad_out[m * PIECE : (m + 1) * PIECE, :] = pieces[m].astype(F32)
    bgrad_out[...] = bgrad[...]


def per_device(history, tiles, tile_row, tile_col, weight, bias, cotangent):
    any_ref = pl.BlockSpec(memory_space=pl.ANY)
    vmem = pl.BlockSpec(memory_space=pltpu.VMEM)
    dma = pltpu.SemaphoreType.DMA
    nodes = history.shape[0]
    act, wgrad, bgrad = pl.pallas_call(
        kernel,
        out_shape=(
            jax.ShapeDtypeStruct((nodes, H), BF16),
            jax.ShapeDtypeStruct((MEM, PIECE, H), BF16),
            jax.ShapeDtypeStruct((1, H), F32),
        ),
        in_specs=[any_ref, any_ref, vmem, vmem, any_ref, vmem, any_ref],
        out_specs=(vmem, vmem, vmem),
        scratch_shapes=[
            pltpu.VMEM((NBLK, BS, H), BF16),
            pltpu.VMEM((TILES + 1, BS, BS), BF16),
            pltpu.VMEM((PAIRS + 1, BS, H), BF16),
            pltpu.VMEM((BS, H), F32),
            pltpu.VMEM((NSEND, BS, H), BF16),
            pltpu.VMEM((8, LANES), I32),
            pltpu.VMEM((8, 128), I32),
            pltpu.SMEM((8, LANES), I32),
            pltpu.SMEM((8, 128), I32),
            pltpu.VMEM((H, H), BF16),
            pltpu.VMEM((OWN * BS, H), BF16),
                pltpu.VMEM((MEM, PIECE, WIDE), BF16),
            pltpu.VMEM((MEM, PIECE, WIDE), BF16),
            pltpu.VMEM((PIECE, WIDE), BF16),
            pltpu.VMEM((GRP, PIECE, WIDE), BF16),
            pltpu.VMEM((MEM, PIECE, H), BF16),
            dma((9,)),
            dma((NSEND,)),
            dma((NBLK,)),
            dma((NSEND,)),
            dma((NSEND,)),
            dma((MEM - 1,)),
            dma((MEM - 1,)),
            dma((GRP - 1,)),
            dma((GRP - 1,)),
            dma((MEM - 1,)),
            dma((MEM - 1,)),
        ],
        compiler_params=pltpu.CompilerParams(
            collective_id=0, has_side_effects=True, vmem_limit_bytes=61 * 2**20
        ),
    )(
        history.reshape(OWN, BS, H),
        tiles,
        tile_row,
        tile_col,
        weight,
        bias.reshape(1, H),
        cotangent,
    )
    act, wgrad, bgrad = pl.pallas_call(
        finish,
        out_shape=(
            jax.ShapeDtypeStruct((nodes, H), BF16),
            jax.ShapeDtypeStruct((H, H), F32),
            jax.ShapeDtypeStruct((1, H), F32),
        ),
        in_specs=[vmem, vmem, vmem],
        out_specs=(vmem, vmem, vmem),
        compiler_params=pltpu.CompilerParams(vmem_limit_bytes=61 * 2**20),
    )(act, wgrad, bgrad)
    return act, wgrad, bgrad.reshape(H)


def solution(mesh):
    both = ("grp", "mem")
    placed = (
        P(both, None),
        P(both, None, None),
        P(both),
        P(both),
        P(),
        P(),
        P(both, None),
    )
    return jax.shard_map(
        per_device,
        mesh=mesh,
        in_specs=placed,
        out_specs=(P(both, None), P(), P()),
        check_vma=False,
    )
```
